32 devices in a mesh: grp: 1, src: 16 (over z, y, x), srf: 2 (over core).
Axes of the slice: x: 2, y: 2, z: 4, core: 2. Of those that a mesh axis runs over, the one named last changes fastest.
Arguments:
- left_traces: bfloat16 [128, 512, 256], P(('grp', 'src'), 'srf'), may hold values from -6 to 6
- right_traces: bfloat16 [2, 256, 512, 256], P('srf', 'src', 'grp'), may hold values from -0.03125 to 0.03125
- surf_map: int32 [512], P(('grp', 'srf')), may hold values from 0 to 255, as said below
- shot_map: int32 [512], P(('grp', 'srf')), may hold values from 0 to 255, as said below
Outputs:
- multiples: bfloat16 [128, 512, 256], P(('grp', 'src'), 'srf')
The draws below stay inside these ranges and needn't reach their ends.
Inputs may be any that keep to these rules, and one draw needn't show every extreme that they name: `surf_map`: each aligned block of 256 entries holds every number of 0 to 255 once. `shot_map`: each aligned block of 256 entries holds every number of 0 to 255 once.
All inputs are finite; a program needn't handle non-finite values.
Results may differ from the reference program's by a relative error of at most 0.0058.
Values may be sent and summed in bfloat16 or wider, within the bound.
A program may use at most 192 MiB of HBM per device.

```python
import math
import jax
import jax.numpy as jnp
from jax import lax

SAMPLES = 256
POINTS = 512
RECEIVERS = 512
BINS = 40
SRC_DEV = 8
SOURCES = 128
HALF_POINTS = 256
N_SRF = 2


def half_permutations(key):
    pieces = [jax.random.permutation(jax.random.fold_in(key, half_index), HALF_POINTS).astype(jnp.int32) for half_index in range(POINTS // HALF_POINTS)]
    return jnp.concatenate(pieces)


def draw_surf_map(key, part):
    key = jax.random.fold_in(key, 11)
    return half_permutations(key)


def draw_shot_map(key, part):
    key = jax.random.fold_in(key, 23)
    return half_permutations(key)


def levels(stream_key, dims, shards, low, top_value):
    def one(position, parts):
        steps = jax.random.uniform(jax.random.fold_in(jax.random.fold_in(stream_key, 6), position), (parts,), jnp.float32, low / len(shards), top_value / len(shards))
        return jnp.repeat(jnp.exp(steps), dims[position] // parts).reshape((-1,) + (1,) * (len(dims) - position - 1))

    gain = one(*shards[0])
    for cut in shards[1:]:
        gain = gain * one(*cut)
    return gain


def normal_values(rng, dims, scale, limit, cuts=(), kind=jnp.bfloat16):
    array = scale * jax.random.normal(rng, dims, jnp.float32)
    if cuts:
        array = array * levels(rng, dims, cuts, -0.22, 0.18)
    return jnp.clip(array, -limit, limit).astype(kind)


def setup_inputs(seed: int = 0, part: int = 0) -> dict:
    arg_keys = jax.random.split(jax.random.key(seed), 5)
    part_keys = jax.random.split(jax.random.fold_in(arg_keys[4], part), 5)
    left_traces = normal_values(part_keys[0], (SOURCES, POINTS, SAMPLES), 1.0, 6.0, ((0, 16), (1, 2)))
    right_traces = normal_values(part_keys[1], (N_SRF, HALF_POINTS, RECEIVERS, SAMPLES), (2 * BINS * POINTS) ** -0.5, 0.03125, ((0, 2), (1, 16)))
    surf_map = draw_surf_map(jax.random.fold_in(jax.random.fold_in(arg_keys[4], part), 71), part)
    shot_map = draw_shot_map(jax.random.fold_in(jax.random.fold_in(arg_keys[4], part), 71), part)
    return dict(left_traces=left_traces, right_traces=right_traces, surf_map=surf_map, shot_map=shot_map)


FULL_ACCURACY = lax.Precision.HIGHEST


def tables(samples, bin_count):
    bin_index = jnp.arange(1, bin_count + 1, dtype=jnp.int32)
    time_index = jnp.arange(samples, dtype=jnp.int32)
    phase_int = (bin_index[:, None] * time_index[None, :]) % samples
    angles = phase_int.astype(jnp.float32) * (2.0 * math.pi / samples)
    forward = jnp.concatenate([jnp.cos(angles), -jnp.sin(angles)], axis=0)
    inverse = forward * (2.0 / samples)
    return forward, inverse


def spectra(traces, forward):
    widened = traces.astype(jnp.float32)
    return jnp.einsum("ct,abt->cab", forward, widened, precision=FULL_ACCURACY).astype(jnp.bfloat16)


def complex_product(left_operand, right_operand):
    left_real_component, left_imaginary = left_operand[:BINS], left_operand[BINS:]
    right_real_component, right_imaginary = right_operand[:BINS], right_operand[BINS:]
    real_component = jnp.einsum("evz,ezh->evh", left_real_component, right_real_component, precision=FULL_ACCURACY) - jnp.einsum("evz,ezh->evh", left_imaginary, right_imaginary, precision=FULL_ACCURACY)
    imaginary_component = jnp.einsum("evz,ezh->evh", left_real_component, right_imaginary, precision=FULL_ACCURACY) + jnp.einsum("evz,ezh->evh", left_imaginary, right_real_component, precision=FULL_ACCURACY)
    return jnp.concatenate([real_component, imaginary_component], axis=0)


def reference(left_traces, right_traces, surf_map, shot_map):
    forward, inverse = tables(SAMPLES, BINS)
    offsets = (jnp.arange(POINTS, dtype=jnp.int32) // HALF_POINTS) * HALF_POINTS
    column_list = (surf_map + offsets).astype(jnp.int32)
    row_list = (shot_map + offsets).astype(jnp.int32)

    def right_half(traces):
        return spectra(traces, forward)

    right_band = lax.map(right_half, right_traces)
    right_band = jnp.transpose(right_band, (1, 0, 2, 3)).reshape(2 * BINS, POINTS, RECEIVERS)
    right_wide = jnp.take(right_band, row_list, axis=1).astype(jnp.float32)

    def one_block(block):
        left_band = spectra(block, forward)
        left_wide = jnp.take(left_band, column_list, axis=2).astype(jnp.float32)
        band = complex_product(left_wide, right_wide)
        signal = jnp.einsum("csr,ct->srt", band, inverse, precision=FULL_ACCURACY)
        return signal.astype(jnp.bfloat16)

    blocks = left_traces.reshape(SOURCES // SRC_DEV, SRC_DEV, POINTS, SAMPLES)
    return lax.map(one_block, blocks).reshape(SOURCES, RECEIVERS, SAMPLES)
```

```python
import functools
import math

import jax
import jax.numpy as jnp
import ml_dtypes
import numpy as np
from jax import lax
from jax.experimental import pallas as pl
from jax.experimental.pallas import tpu as pltpu
from jax.sharding import PartitionSpec as P

BINS = 40
GROUP = 8
SLOTS = BINS // GROUP
ROW_TILE = 16
F32 = jnp.float32
BF16 = jnp.bfloat16


def split(table):
    high = table.astype(ml_dtypes.bfloat16)
    low = (table - high.astype(np.float64)).astype(ml_dtypes.bfloat16)
    return np.concatenate([high, low], axis=0)


def tables(samples):
    phase = np.arange(1, BINS + 1)[:, None] * np.arange(samples)[None, :] % samples
    angles = phase * (2.0 * math.pi / samples)
    forward = np.stack([np.cos(angles), -np.sin(angles)], axis=1).reshape(2 * BINS, samples)
    return split(forward), split(forward * (2.0 / samples))


def exchange(n, right, left, out, r_in, l_in, part, c_in, z_out, z_in, f_out, f_in,
             r_send, r_recv, l_send, l_recv, c_send, c_recv, z_send, z_recv, f_send, f_recv):
    teams = n // GROUP
    me = lax.axis_index("src")
    core = lax.axis_index("srf")
    other = 1 - core
    team = me // GROUP
    place = me % GROUP
    rows = GROUP * ROW_TILE
    half = part.shape[-1]

    barrier = pltpu.get_barrier_semaphore()

    def greet(d, carry):
        pl.semaphore_signal(barrier, inc=1, device_id={"src": lax.rem(me + d, n)})
        return carry

    lax.fori_loop(1, n, greet, 0)
    pl.semaphore_signal(barrier, inc=1, device_id={"srf": other})
    pl.semaphore_wait(barrier, n)

    def l_copy(d):
        to = lax.rem(me + d, n)
        return pltpu.make_async_remote_copy(
            left.at[to], l_in.at[me], l_send.at[d], l_recv.at[d], device_id={"src": to})

    def r_copy(b, d):
        to = lax.rem(place + d, GROUP)
        return pltpu.make_async_remote_copy(
            right.at[to, b], r_in.at[b, :, place], r_send.at[b, d], r_recv.at[b, d],
            device_id={"src": team * GROUP + to})

    def c_copy(b):
        return pltpu.make_async_remote_copy(
            part.at[b, other], c_in.at[b], c_send.at[b], c_recv.at[b], device_id={"srf": other})

    def z_copy(b, d):
        to = lax.rem(team + d, teams)
        return pltpu.make_async_remote_copy(
            z_out.at[b, to], z_in.at[b, d], z_send.at[b, d], z_recv.at[b, d],
            device_id={"src": to * GROUP + place})

    def f_copy(b, d):
        to = lax.rem(place + d, GROUP)
        return pltpu.make_async_remote_copy(
            f_out.at[b, to], f_in.at[place, b], f_send.at[b, d], f_recv.at[b, d],
            device_id={"src": team * GROUP + to})

    def start_left(d, carry):
        l_copy(d).start()
        return carry

    lax.fori_loop(1, n, start_left, 0)
    for b in range(SLOTS):
        for d in range(1, GROUP):
            r_copy(b, d).start()
    l_in[me] = left[me]
    for b in range(SLOTS):
        r_in[b, :, place] = right[place, b]

    def wait_left(d, carry):
        l_copy(d).wait_recv()
        return carry

    lax.fori_loop(1, n, wait_left, 0)

    def multiply(b):
        for d in range(1, GROUP):
            r_copy(b, d).wait_recv()
        straight = l_in[:, b].reshape(n * ROW_TILE, rows)
        wide = straight.astype(F32).reshape(n, 2, ROW_TILE // 2, rows)
        turned = jnp.concatenate([-wide[:, 1:2], wide[:, 0:1]], axis=1)
        turned = turned.reshape(n * ROW_TILE, rows).astype(BF16)
        real = r_in[b, 0].reshape(rows, 2 * half)
        imag = r_in[b, 1].reshape(rows, 2 * half)
        total = jnp.dot(straight, real, preferred_element_type=F32)
        total += jnp.dot(turned, imag, preferred_element_type=F32)
        part[b, 0] = total[:, :half]
        part[b, 1] = total[:, half:]
        c_copy(b).start()

    def add_cores(b):
        c_copy(b).wait_recv()
        total = part[b, core] + c_in[b]
        part[b, core] = total
        z_out[b] = total.astype(BF16).reshape(teams, rows, half)
        for d in range(1, teams):
            z_copy(b, d).start()

    def add_teams(b):
        total = part[b, core, pl.ds(pl.multiple_of(team * rows, rows), rows), :]
        for d in range(1, teams):
            z_copy(b, d).wait_recv()
            total += z_in[b, d].astype(F32)
        f_out[b] = total.astype(BF16).reshape(GROUP, ROW_TILE, half)
        for d in range(1, GROUP):
            f_copy(b, d).start()
        f_in[place, b] = f_out[b, place]

    for step in range(SLOTS + 2):
        if step < SLOTS:
            multiply(step)
        if 0 <= step - 1 < SLOTS:
            add_cores(step - 1)
        if 0 <= step - 2 < SLOTS:
            add_teams(step - 2)
    for b in range(SLOTS):
        for d in range(1, GROUP):
            f_copy(b, d).wait_recv()
    out[...] = f_in[...]

    def end_left(d, carry):
        l_copy(d).wait_send()
        return carry

    lax.fori_loop(1, n, end_left, 0)
    for b in range(SLOTS):
        c_copy(b).wait_send()
        for d in range(1, GROUP):
            r_copy(b, d).wait_send()
            f_copy(b, d).wait_send()
        for d in range(1, teams):
            z_copy(b, d).wait_send()


def band_of(n, right, left):
    teams = n // GROUP
    rows = GROUP * ROW_TILE
    receivers = right.shape[-1]
    half = receivers // 2
    dma = pltpu.SemaphoreType.DMA
    vmem = pl.BlockSpec(memory_space=pltpu.VMEM)
    return pl.pallas_call(
        functools.partial(exchange, n),
        out_shape=jax.ShapeDtypeStruct((GROUP, SLOTS, ROW_TILE, half), BF16),
        in_specs=[vmem, vmem],
        out_specs=vmem,
        scratch_shapes=[
            pltpu.VMEM((SLOTS, 2, GROUP, ROW_TILE, receivers), BF16),
            pltpu.VMEM((n, SLOTS, ROW_TILE, rows), BF16),
            pltpu.VMEM((SLOTS, 2, n * ROW_TILE, half), F32),
            pltpu.VMEM((SLOTS, n * ROW_TILE, half), F32),
            pltpu.VMEM((SLOTS, teams, rows, half), BF16),
            pltpu.VMEM((SLOTS, teams, rows, half), BF16),
            pltpu.VMEM((SLOTS, GROUP, ROW_TILE, half), BF16),
            pltpu.VMEM((GROUP, SLOTS, ROW_TILE, half), BF16),
            dma((SLOTS, GROUP)), dma((SLOTS, GROUP)),
            dma((n,)), dma((n,)),
            dma((SLOTS,)), dma((SLOTS,)),
            dma((SLOTS, teams)), dma((SLOTS, teams)),
            dma((SLOTS, GROUP)), dma((SLOTS, GROUP)),
        ],
        compiler_params=pltpu.CompilerParams(
            collective_id=0, has_side_effects=True, vmem_limit_bytes=48 * 2**20),
        cost_estimate=pl.CostEstimate(
            flops=2 * SLOTS * n * ROW_TILE * 2 * rows * receivers,
            bytes_accessed=2 * right.size * 2, transcendentals=0),
    )(right, left)


def local(n, left_traces, right_traces, surf_map, shot_map):
    sources, half_size, samples = left_traces.shape
    row_count, receivers = right_traces.shape[1:3]
    teams = n // GROUP
    values = 2 * BINS
    forward, inverse = tables(samples)

    def spectra(traces):
        both = [
            jnp.einsum("ct,abt->cab", forward[part], traces, preferred_element_type=F32)
            for part in (slice(None, values), slice(values, None))
        ]
        return (both[0] + both[1]).astype(BF16)

    pad = ROW_TILE - row_count
    right = spectra(right_traces[0])
    if pad:
        right = jnp.pad(right, ((0, 0), (0, pad), (0, 0)))
    right = right.reshape(GROUP, SLOTS, 2, ROW_TILE, receivers)

    columns = jnp.arange(half_size, dtype=jnp.int32)
    surf_hot = (surf_map[:, None] == columns[None, :]).astype(BF16)
    shot_hot = (shot_map[:, None] == columns[None, :]).astype(BF16)
    move = jnp.einsum("jk,jq->kq", surf_hot, shot_hot, preferred_element_type=F32).astype(BF16)
    left = spectra(left_traces)
    left = jnp.einsum("csk,kq->csq", left, move, preferred_element_type=F32).astype(BF16)
    left = left.reshape(GROUP, SLOTS, 2, sources, teams, GROUP, row_count)
    if pad:
        left = jnp.pad(left, ((0, 0),) * 6 + ((0, pad),))
    left = left.transpose(4, 0, 1, 2, 3, 5, 6).reshape(n, SLOTS, ROW_TILE, GROUP * ROW_TILE)

    band = band_of(n, right, left).reshape(BINS * 2, sources, receivers // 2)
    result = [
        jnp.einsum("csr,ct->srt", band, inverse[part], preferred_element_type=F32)
        for part in (slice(None, values), slice(values, None))
    ]
    return (result[0] + result[1]).astype(BF16)


def solution(mesh):
    in_specs = (
        P(("grp", "src"), "srf", None),
        P("srf", "src", "grp", None),
        P(("grp", "srf")),
        P(("grp", "srf")),
    )
    out_specs = P(("grp", "src"), "srf", None)
    body = functools.partial(local, mesh.shape["src"])
    return jax.shard_map(body, mesh=mesh, in_specs=in_specs, out_specs=out_specs, check_vma=False)
```

```python
import functools
import math

import jax
import jax.numpy as jnp
import ml_dtypes
import numpy as np
from jax import lax
from jax.experimental import pallas as pl
from jax.experimental.pallas import tpu as pltpu
from jax.sharding import PartitionSpec as P

BINS = 40
GROUP = 8
SLOTS = BINS // GROUP
ROW_TILE = 16
LANES = 128
F32 = jnp.float32
BF16 = jnp.bfloat16


def split(table):
    high = table.astype(ml_dtypes.bfloat16)
    low = (table - high.astype(np.float64)).astype(ml_dtypes.bfloat16)
    return np.concatenate([high, low], axis=0)


def tables(samples):
    phase = np.arange(1, BINS + 1)[:, None] * np.arange(samples)[None, :] % samples
    angles = phase * (2.0 * math.pi / samples)
    forward = np.stack([np.cos(angles), -np.sin(angles)], axis=1).reshape(2 * BINS, samples)
    return split(forward), split(forward * (2.0 / samples))


NT = (((1,), (1,)), ((), ()))


def exchange(n, left_ref, right_ref, surf_ref, shot_ref, table_ref, out, traces, lines, right, left,
             r_in, l_in, part, c_in, z_out, z_in, f_out, f_in, fetch_sem,
             r_send, r_recv, l_send, l_recv, c_send, c_recv, z_send, z_recv, f_send, f_recv):
    teams = n // GROUP
    me = lax.axis_index("src")
    core = lax.axis_index("srf")
    other = 1 - core
    team = me // GROUP
    place = me % GROUP
    rows = GROUP * ROW_TILE
    half = part.shape[-1]
    values = 2 * BINS
    sources, half_size, _ = left_ref.shape
    row_count, receivers = right_ref.shape[1:3]

    barrier = pltpu.get_barrier_semaphore()

    def greet(d, carry):
        pl.semaphore_signal(barrier, inc=1, device_id={"src": lax.rem(me + d, n)})
        return carry

    lax.fori_loop(1, n, greet, 0)
    pl.semaphore_signal(barrier, inc=1, device_id={"srf": other})
    fetch = pltpu.make_async_copy(right_ref.at[0], traces, fetch_sem)
    fetch.start()

    def spectrum(block):
        both = lax.dot_general(table_ref[...], block, NT, preferred_element_type=F32)
        return (both[:values] + both[values:]).astype(BF16)

    at = lax.broadcasted_iota(jnp.int32, (half_size, half_size), 0)
    surf_hot = (at == surf_ref[...]).astype(F32).astype(BF16)
    spot = lax.broadcasted_iota(jnp.int32, (teams * rows, half_size), 0)
    shot = shot_ref[...]
    shot_spot = shot // row_count * ROW_TILE + shot % row_count
    shot_hot = (spot == shot_spot).astype(F32).astype(BF16)
    move = lax.dot_general(surf_hot, shot_hot, NT, preferred_element_type=F32).astype(BF16)
    for s in range(sources):
        moved = jnp.dot(spectrum(left_ref[s]), move, preferred_element_type=F32)
        for t in range(teams):
            lines[t, pl.ds(s, values, stride=sources), :] = moved[:, t * rows:(t + 1) * rows]
    for t in range(teams):
        block = lines[t, :values * sources].astype(BF16)
        left[t * GROUP:(t + 1) * GROUP] = block.reshape(GROUP, SLOTS, ROW_TILE, rows)

    pl.semaphore_wait(barrier, n)

    def l_copy(d):
        to = lax.rem(me + d, n)
        return pltpu.make_async_remote_copy(
            left.at[to], l_in.at[me], l_send.at[d], l_recv.at[d], device_id={"src": to})

    def r_copy(b, d):
        to = lax.rem(place + d, GROUP)
        return pltpu.make_async_remote_copy(
            right.at[to, b], r_in.at[b, :, place], r_send.at[b, d], r_recv.at[b, d],
            device_id={"src": team * GROUP + to})

    def c_copy(b):
        return pltpu.make_async_remote_copy(
            part.at[b, other], c_in.at[b], c_send.at[b], c_recv.at[b], device_id={"srf": other})

    def z_copy(b, d):
        to = lax.rem(team + d, teams)
        return pltpu.make_async_remote_copy(
            z_out.at[b, to], z_in.at[b, d], z_send.at[b, d], z_recv.at[b, d],
            device_id={"src": to * GROUP + place})

    def f_copy(b, d):
        to = lax.rem(place + d, GROUP)
        return pltpu.make_async_remote_copy(
            f_out.at[b, to], f_in.at[place, b], f_send.at[b, d], f_recv.at[b, d],
            device_id={"src": team * GROUP + to})

    def start_left(d, carry):
        l_copy(d).start()
        return carry

    lax.fori_loop(1, n, start_left, 0)

    fetch.wait()
    if row_count < ROW_TILE:
        lines[...] = jnp.zeros_like(lines)
    for q in range(row_count):
        bands = spectrum(traces[q]).astype(F32)
        for t in range(receivers // LANES):
            lines[t, pl.ds(q, values, stride=ROW_TILE), :] = bands[:, t * LANES:(t + 1) * LANES]
    for t in range(receivers // LANES):
        block = lines[t].astype(BF16).reshape(GROUP, SLOTS, 2, ROW_TILE, LANES)
        right[..., t * LANES:(t + 1) * LANES] = block
    for b in range(SLOTS):
        for d in range(1, GROUP):
            r_copy(b, d).start()
    l_in[me] = left[me]
    for b in range(SLOTS):
        r_in[b, :, place] = right[place, b]

    def wait_left(d, carry):
        l_copy(d).wait_recv()
        return carry

    lax.fori_loop(1, n, wait_left, 0)

    def multiply(b):
        for d in range(1, GROUP):
            r_copy(b, d).wait_recv()
        straight = l_in[:, b].reshape(n * ROW_TILE, rows)
        wide = straight.astype(F32).reshape(n, 2, ROW_TILE // 2, rows)
        turned = jnp.concatenate([-wide[:, 1:2], wide[:, 0:1]], axis=1)
        turned = turned.reshape(n * ROW_TILE, rows).astype(BF16)
        real = r_in[b, 0].reshape(rows, 2 * half)
        imag = r_in[b, 1].reshape(rows, 2 * half)
        total = jnp.dot(straight, real, preferred_element_type=F32)
        total += jnp.dot(turned, imag, preferred_element_type=F32)
        part[b, 0] = total[:, :half]
        part[b, 1] = total[:, half:]
        c_copy(b).start()

    def add_cores(b):
        c_copy(b).wait_recv()
        total = part[b, core] + c_in[b]
        part[b, core] = total
        z_out[b] = total.astype(BF16).reshape(teams, rows, half)
        for d in range(1, teams):
            z_copy(b, d).start()

    def add_teams(b):
        total = part[b, core, pl.ds(pl.multiple_of(team * rows, rows), rows), :]
        for d in range(1, teams):
            z_copy(b, d).wait_recv()
            total += z_in[b, d].astype(F32)
        f_out[b] = total.astype(BF16).reshape(GROUP, ROW_TILE, half)
        for d in range(1, GROUP):
            f_copy(b, d).start()
        f_in[place, b] = f_out[b, place]

    for step in range(SLOTS + 2):
        if step < SLOTS:
            multiply(step)
        if 0 <= step - 1 < SLOTS:
            add_cores(step - 1)
        if 0 <= step - 2 < SLOTS:
            add_teams(step - 2)
    for b in range(SLOTS):
        for d in range(1, GROUP):
            f_copy(b, d).wait_recv()
    out[...] = f_in[...]

    def end_left(d, carry):
        l_copy(d).wait_send()
        return carry

    lax.fori_loop(1, n, end_left, 0)
    for b in range(SLOTS):
        c_copy(b).wait_send()
        for d in range(1, GROUP):
            r_copy(b, d).wait_send()
            f_copy(b, d).wait_send()
        for d in range(1, teams):
            z_copy(b, d).wait_send()


def band_of(n, left, right, surf_map, shot_map, table):
    teams = n // GROUP
    rows = GROUP * ROW_TILE
    receivers = right.shape[2]
    half = receivers // 2
    dma = pltpu.SemaphoreType.DMA
    vmem = pl.BlockSpec(memory_space=pltpu.VMEM)
    return pl.pallas_call(
        functools.partial(exchange, n),
        out_shape=jax.ShapeDtypeStruct((GROUP, SLOTS, ROW_TILE, half), BF16),
        in_specs=[vmem, pl.BlockSpec(memory_space=pl.ANY), vmem, vmem, vmem],
        out_specs=vmem,
        scratch_shapes=[
            pltpu.VMEM(right.shape[1:], BF16),
            pltpu.VMEM((max(teams, receivers // LANES), 2 * BINS * ROW_TILE, LANES), F32),
            pltpu.VMEM((GROUP, SLOTS, 2, ROW_TILE, receivers), BF16),
            pltpu.VMEM((n, SLOTS, ROW_TILE, rows), BF16),
            pltpu.VMEM((SLOTS, 2, GROUP, ROW_TILE, receivers), BF16),
            pltpu.VMEM((n, SLOTS, ROW_TILE, rows), BF16),
            pltpu.VMEM((SLOTS, 2, n * ROW_TILE, half), F32),
            pltpu.VMEM((SLOTS, n * ROW_TILE, half), F32),
            pltpu.VMEM((SLOTS, teams, rows, half), BF16),
            pltpu.VMEM((SLOTS, teams, rows, half), BF16),
            pltpu.VMEM((SLOTS, GROUP, ROW_TILE, half), BF16),
            pltpu.VMEM((GROUP, SLOTS, ROW_TILE, half), BF16),
            dma(()),
            dma((SLOTS, GROUP)), dma((SLOTS, GROUP)),
            dma((n,)), dma((n,)),
            dma((SLOTS,)), dma((SLOTS,)),
            dma((SLOTS, teams)), dma((SLOTS, teams)),
            dma((SLOTS, GROUP)), dma((SLOTS, GROUP)),
        ],
        compiler_params=pltpu.CompilerParams(
            collective_id=0, has_side_effects=True, vmem_limit_bytes=48 * 2**20),
        cost_estimate=pl.CostEstimate(
            flops=2 * SLOTS * n * ROW_TILE * 2 * rows * receivers,
            bytes_accessed=2 * right.size * 2, transcendentals=0),
    )(left, right, surf_map, shot_map, table)


def local(n, left_traces, right_traces, surf_map, shot_map):
    sources, _, samples = left_traces.shape
    receivers = right_traces.shape[2]
    values = 2 * BINS
    forward, inverse = tables(samples)
    band = band_of(n, left_traces, right_traces, surf_map[None], shot_map[None], jnp.asarray(forward))
    band = band.reshape(values, sources, receivers // 2)
    result = [
        jnp.einsum("csr,ct->srt", band, inverse[part], preferred_element_type=F32)
        for part in (slice(None, values), slice(values, None))
    ]
    return (result[0] + result[1]).astype(BF16)


def solution(mesh):
    in_specs = (
        P(("grp", "src"), "srf", None),
        P("srf", "src", "grp", None),
        P(("grp", "srf")),
        P(("grp", "srf")),
    )
    out_specs = P(("grp", "src"), "srf", None)
    body = functools.partial(local, mesh.shape["src"])
    return jax.shard_map(body, mesh=mesh, in_specs=in_specs, out_specs=out_specs, check_vma=False)
```

```python
import functools
import math

import jax
import jax.numpy as jnp
import ml_dtypes
import numpy as np
from jax import lax
from jax.experimental import pallas as pl
from jax.experimental.pallas import tpu as pltpu
from jax.sharding import PartitionSpec as P

BINS = 40
GROUP = 8
SLOTS = BINS // GROUP
ROW_TILE = 16
LANES = 128
FIRST = 3
EARLY = 6
AHEAD = 4
GAP = 3
F32 = jnp.float32
BF16 = jnp.bfloat16


def split(table):
    high = table.astype(ml_dtypes.bfloat16)
    low = (table - high.astype(np.float64)).astype(ml_dtypes.bfloat16)
    return np.concatenate([high, low], axis=0)


def tables(samples):
    phase = np.arange(1, BINS + 1)[:, None] * np.arange(samples)[None, :] % samples
    angles = phase * (2.0 * math.pi / samples)
    forward = np.stack([np.cos(angles), -np.sin(angles)], axis=1).reshape(2 * BINS, samples)
    return split(forward), split(forward * (2.0 / samples))


NT = (((1,), (1,)), ((), ()))


def exchange(n, left_hbm, right_hbm, surf_hbm, shot_hbm, table_hbm, out, left_ref, traces, surf_ref,
             shot_ref, table_ref, lines, right, left,
             r_in, l_in, l_turn, part, c_in, z_out, z_in, f_out, f_in, fetch_sem,
             r_send, r_recv, l_send, l_recv, c_send, c_recv, z_send, z_recv, f_send, f_recv):
    teams = n // GROUP
    me = lax.axis_index("src")
    core = lax.axis_index("srf")
    other = 1 - core
    team = me // GROUP
    place = me % GROUP
    rows = GROUP * ROW_TILE
    half = part.shape[-1]
    values = 2 * BINS
    sources, half_size, _ = left_ref.shape
    row_count, receivers = right_hbm.shape[1:3]

    pairs = [(surf_hbm, surf_ref), (shot_hbm, shot_ref), (table_hbm, table_ref), (left_hbm, left_ref),
             (right_hbm.at[0], traces)]
    fetches = [pltpu.make_async_copy(a, b, fetch_sem.at[i]) for i, (a, b) in enumerate(pairs)]
    for fetch in fetches:
        fetch.start()

    barrier = pltpu.get_barrier_semaphore()

    def greet(d, carry):
        pl.semaphore_signal(barrier, inc=1, device_id={"src": lax.rem(me + d, n)})
        return carry

    lax.fori_loop(1, n, greet, 0)
    pl.semaphore_signal(barrier, inc=1, device_id={"srf": other})
    def spectrum(block):
        both = lax.dot_general(table_ref[...], block, NT, preferred_element_type=F32)
        return (both[:values] + both[values:]).astype(BF16)

    for fetch in fetches[:4]:
        fetch.wait()
    at = lax.broadcasted_iota(jnp.int32, (half_size, half_size), 0)
    surf_hot = (at == surf_ref[...]).astype(F32).astype(BF16)
    spot = lax.broadcasted_iota(jnp.int32, (teams * rows, half_size), 0)
    shot = shot_ref[...]
    shot_spot = shot // row_count * ROW_TILE + shot % row_count
    shot_hot = (spot == shot_spot).astype(F32).astype(BF16)
    move = lax.dot_general(surf_hot, shot_hot, NT, preferred_element_type=F32).astype(BF16)
    for s in range(sources):
        moved = jnp.dot(spectrum(left_ref[s]), move, preferred_element_type=F32)
        for t in range(teams):
            lines[t, pl.ds(s, values, stride=sources), :] = moved[:, t * rows:(t + 1) * rows]
    for t in range(teams):
        block = lines[t, :values * sources].astype(BF16)
        left[t * GROUP:(t + 1) * GROUP] = block.reshape(GROUP, SLOTS, ROW_TILE, rows)

    pl.semaphore_wait(barrier, n)

    def l_copy(d):
        to = lax.rem(me + d, n)
        return pltpu.make_async_remote_copy(
            left.at[to], l_in.at[me], l_send.at[d], l_recv.at[d], device_id={"src": to})

    units = [(part_index, b) for part_index in range(2) for b in range(SLOTS)]

    def r_copy(u, d):
        to = lax.rem(place + d, GROUP)
        side, b = units[u]
        return pltpu.make_async_remote_copy(
            right.at[side, to, b], r_in.at[side, b, :, place], r_send.at[u, d], r_recv.at[u, d],
            device_id={"src": team * GROUP + to})

    def start_right(u):
        for d in range(1, GROUP):
            r_copy(u, d).start()

    def c_copy(b):
        return pltpu.make_async_remote_copy(
            part.at[b, other], c_in.at[b], c_send.at[b], c_recv.at[b], device_id={"srf": other})

    def z_copy(b, d):
        to = lax.rem(team + d, teams)
        return pltpu.make_async_remote_copy(
            z_out.at[b, to], z_in.at[b, d], z_send.at[b, d], z_recv.at[b, d],
            device_id={"src": to * GROUP + place})

    def f_copy(b, d):
        to = lax.rem(place + d, GROUP)
        return pltpu.make_async_remote_copy(
            f_out.at[b, to], f_in.at[place, b], f_send.at[b, d], f_recv.at[b, d],
            device_id={"src": team * GROUP + to})

    def start_left(d, carry):
        l_copy(d).start()
        return carry

    lax.fori_loop(1, n, start_left, 0)

    fetches[4].wait()
    if row_count < ROW_TILE:
        lines[...] = jnp.zeros_like(lines)
    for side in range(2):
        for q in range(row_count):
            bands = spectrum(traces[q, side * half:(side + 1) * half]).astype(F32)
            for t in range(half // LANES):
                lines[side * (half // LANES) + t, pl.ds(q, values, stride=ROW_TILE), :] = (
                    bands[:, t * LANES:(t + 1) * LANES])
        for t in range(half // LANES):
            block = lines[side * (half // LANES) + t].astype(BF16)
            right[side, ..., t * LANES:(t + 1) * LANES] = block.reshape(
                GROUP, SLOTS, 2, ROW_TILE, LANES)
        for u in range(FIRST) if side == 0 else range(FIRST, EARLY):
            start_right(u)
        for b in range(SLOTS):
            r_in[side, b, :, place] = right[side, place, b]
    l_in[me] = left[me]

    def wait_left(d, carry):
        l_copy(d).wait_recv()
        return carry

    lax.fori_loop(1, n, wait_left, 0)
    for b in range(SLOTS):
        wide = l_in[:, b].astype(F32).reshape(n, 2, ROW_TILE // 2, rows)
        turned = jnp.concatenate([-wide[:, 1:2], wide[:, 0:1]], axis=1)
        l_turn[b] = turned.reshape(n * ROW_TILE, rows).astype(BF16)

    def multiply(u):
        side, b = units[u]
        for d in range(1, GROUP):
            r_copy(u, d).wait_recv()
        if EARLY <= u + AHEAD < len(units):
            start_right(u + AHEAD)
        straight = l_in[:, b].reshape(n * ROW_TILE, rows)
        real = r_in[side, b, 0].reshape(rows, half)
        imag = r_in[side, b, 1].reshape(rows, half)
        total = jnp.dot(straight, real, preferred_element_type=F32)
        part[b, side] = total + jnp.dot(l_turn[b], imag, preferred_element_type=F32)

        @pl.when(core != side)
        def _():
            c_copy(b).start()

    def add_cores(b):
        c_copy(b).wait_recv()
        total = part[b, core] + c_in[b]
        part[b, core] = total
        z_out[b] = total.astype(BF16).reshape(teams, rows, half)
        for d in range(1, teams):
            z_copy(b, d).start()

    def add_teams(b):
        total = part[b, core, pl.ds(pl.multiple_of(team * rows, rows), rows), :]
        for d in range(1, teams):
            z_copy(b, d).wait_recv()
            total += z_in[b, d].astype(F32)
        f_out[b] = total.astype(BF16).reshape(GROUP, ROW_TILE, half)
        for d in range(1, GROUP):
            f_copy(b, d).start()
        f_in[place, b] = f_out[b, place]

    for step in range(len(units) + GAP):
        if step < len(units):
            multiply(step)
        for lag, work in ((1, add_cores), (GAP, add_teams)):
            if 0 <= step - lag < len(units):
                side, b = units[step - lag]
                pl.when(core == side)(functools.partial(work, b))
    for b in range(SLOTS):
        for d in range(1, GROUP):
            f_copy(b, d).wait_recv()
    out[...] = f_in[...]

    def end_left(d, carry):
        l_copy(d).wait_send()
        return carry

    lax.fori_loop(1, n, end_left, 0)
    for b in range(SLOTS):
        c_copy(b).wait_send()
        for d in range(1, GROUP):
            r_copy(b, d).wait_send()
            r_copy(b + SLOTS, d).wait_send()
            f_copy(b, d).wait_send()
        for d in range(1, teams):
            z_copy(b, d).wait_send()


def band_of(n, left, right, surf_map, shot_map, table):
    teams = n // GROUP
    rows = GROUP * ROW_TILE
    receivers = right.shape[2]
    half = receivers // 2
    dma = pltpu.SemaphoreType.DMA
    vmem = pl.BlockSpec(memory_space=pltpu.VMEM)
    return pl.pallas_call(
        functools.partial(exchange, n),
        out_shape=jax.ShapeDtypeStruct((GROUP, SLOTS, ROW_TILE, half), BF16),
        in_specs=[pl.BlockSpec(memory_space=pltpu.HBM)] * 5,
        out_specs=vmem,
        scratch_shapes=[
            pltpu.VMEM(left.shape, BF16),
            pltpu.VMEM(right.shape[1:], BF16),
            pltpu.VMEM(surf_map.shape, jnp.int32),
            pltpu.VMEM(shot_map.shape, jnp.int32),
            pltpu.VMEM(table.shape, BF16),
            pltpu.VMEM((max(teams, receivers // LANES), 2 * BINS * ROW_TILE, LANES), F32),
            pltpu.VMEM((2, GROUP, SLOTS, 2, ROW_TILE, half), BF16),
            pltpu.VMEM((n, SLOTS, ROW_TILE, rows), BF16),
            pltpu.VMEM((2, SLOTS, 2, GROUP, ROW_TILE, half), BF16),
            pltpu.VMEM((n, SLOTS, ROW_TILE, rows), BF16),
            pltpu.VMEM((SLOTS, n * ROW_TILE, rows), BF16),
            pltpu.VMEM((SLOTS, 2, n * ROW_TILE, half), F32),
            pltpu.VMEM((SLOTS, n * ROW_TILE, half), F32),
            pltpu.VMEM((SLOTS, teams, rows, half), BF16),
            pltpu.VMEM((SLOTS, teams, rows, half), BF16),
            pltpu.VMEM((SLOTS, GROUP, ROW_TILE, half), BF16),
            pltpu.VMEM((GROUP, SLOTS, ROW_TILE, half), BF16),
            dma((5,)),
            dma((2 * SLOTS, GROUP)), dma((2 * SLOTS, GROUP)),
            dma((n,)), dma((n,)),
            dma((SLOTS,)), dma((SLOTS,)),
            dma((SLOTS, teams)), dma((SLOTS, teams)),
            dma((SLOTS, GROUP)), dma((SLOTS, GROUP)),
        ],
        compiler_params=pltpu.CompilerParams(
            collective_id=0, has_side_effects=True, vmem_limit_bytes=48 * 2**20),
        cost_estimate=pl.CostEstimate(
            flops=2 * SLOTS * n * ROW_TILE * 2 * rows * receivers,
            bytes_accessed=2 * right.size * 2, transcendentals=0),
    )(left, right, surf_map, shot_map, table)


def local(n, left_traces, right_traces, surf_map, shot_map):
    sources, _, samples = left_traces.shape
    receivers = right_traces.shape[2]
    values = 2 * BINS
    forward, inverse = tables(samples)
    band = band_of(n, left_traces, right_traces, surf_map[None], shot_map[None], jnp.asarray(forward))
    band = band.reshape(values, sources, receivers // 2)
    result = [
        jnp.einsum("csr,ct->srt", band, inverse[part], preferred_element_type=F32)
        for part in (slice(None, values), slice(values, None))
    ]
    return (result[0] + result[1]).astype(BF16)


def solution(mesh):
    in_specs = (
        P(("grp", "src"), "srf", None),
        P("srf", "src", "grp", None),
        P(("grp", "srf")),
        P(("grp", "srf")),
    )
    out_specs = P(("grp", "src"), "srf", None)
    body = functools.partial(local, mesh.shape["src"])
    return jax.shard_map(body, mesh=mesh, in_specs=in_specs, out_specs=out_specs, check_vma=False)
```

```python
import functools
import math

import jax
import jax.numpy as jnp
import ml_dtypes
import numpy as np
from jax import lax
from jax.experimental import pallas as pl
from jax.experimental.pallas import tpu as pltpu
from jax.sharding import PartitionSpec as P

BINS = 40
GROUP = 8
SLOTS = BINS // GROUP
ROW_TILE = 16
LANES = 128
FIRST = 2
EARLY = 4
AHEAD = 2
GAP = 3
F32 = jnp.float32
BF16 = jnp.bfloat16


def split(table):
    high = table.astype(ml_dtypes.bfloat16)
    low = (table - high.astype(np.float64)).astype(ml_dtypes.bfloat16)
    return np.concatenate([high, low], axis=0)


def tables(samples):
    phase = np.arange(1, BINS + 1)[:, None] * np.arange(samples)[None, :] % samples
    angles = phase * (2.0 * math.pi / samples)
    forward = np.stack([np.cos(angles), -np.sin(angles)], axis=1).reshape(2 * BINS, samples)
    return split(forward), split(forward * (2.0 / samples))


NT = (((1,), (1,)), ((), ()))


def exchange(n, left_hbm, right_hbm, surf_hbm, shot_hbm, table_hbm, out, left_ref, traces, surf_ref,
             shot_ref, table_ref, lines, right, left,
             r_in, l_in, l_turn, part, c_out, c_in, z_out, z_in, f_out, f_in, fetch_sem,
             r_send, r_recv, l_send, l_recv, c_send, c_recv, z_send, z_recv, f_send, f_recv):
    teams = n // GROUP
    me = lax.axis_index("src")
    core = lax.axis_index("srf")
    other = 1 - core
    team = me // GROUP
    place = me % GROUP
    rows = GROUP * ROW_TILE
    half = part.shape[-1]
    values = 2 * BINS
    sources, half_size, _ = left_ref.shape
    row_count, receivers = right_hbm.shape[1:3]

    pairs = [(surf_hbm, surf_ref), (shot_hbm, shot_ref), (table_hbm, table_ref), (left_hbm, left_ref),
             (right_hbm.at[0], traces)]
    fetches = [pltpu.make_async_copy(a, b, fetch_sem.at[i]) for i, (a, b) in enumerate(pairs)]
    for fetch in fetches:
        fetch.start()

    barrier = pltpu.get_barrier_semaphore()

    def greet(d, carry):
        pl.semaphore_signal(barrier, inc=1, device_id={"src": lax.rem(me + d, n)})
        return carry

    lax.fori_loop(1, n, greet, 0)
    pl.semaphore_signal(barrier, inc=1, device_id={"srf": other})
    def spectrum(block):
        both = lax.dot_general(table_ref[...], block, NT, preferred_element_type=F32)
        return (both[:values] + both[values:]).astype(BF16)

    for fetch in fetches[:4]:
        fetch.wait()
    at = lax.broadcasted_iota(jnp.int32, (half_size, half_size), 0)
    surf_hot = (at == surf_ref[...]).astype(F32).astype(BF16)
    spot = lax.broadcasted_iota(jnp.int32, (teams * rows, half_size), 0)
    shot = shot_ref[...]
    shot_spot = shot // row_count * ROW_TILE + shot % row_count
    shot_hot = (spot == shot_spot).astype(F32).astype(BF16)
    move = lax.dot_general(surf_hot, shot_hot, NT, preferred_element_type=F32).astype(BF16)
    for s in range(sources):
        moved = jnp.dot(spectrum(left_ref[s]), move, preferred_element_type=F32)
        for t in range(teams):
            lines[t, pl.ds(s, values, stride=sources), :] = moved[:, t * rows:(t + 1) * rows]
    for t in range(teams):
        block = lines[t, :values * sources].astype(BF16)
        left[t * GROUP:(t + 1) * GROUP] = block.reshape(GROUP, SLOTS, ROW_TILE, rows)

    pl.semaphore_wait(barrier, n)

    def l_copy(d):
        to = lax.rem(me + d, n)
        return pltpu.make_async_remote_copy(
            left.at[to], l_in.at[me], l_send.at[d], l_recv.at[d], device_id={"src": to})

    units = [(part_index, b) for part_index in range(2) for b in range(SLOTS)]

    def partner(d):
        return sum((place // bit % 2 + d // bit % 2) % 2 * bit for bit in (1, 2, 4))

    def r_copy(u, d):
        to = partner(d)
        side, b = units[u]
        return pltpu.make_async_remote_copy(
            right.at[side, to, b], r_in.at[side, b, :, place], r_send.at[u, d], r_recv.at[u, d],
            device_id={"src": team * GROUP + to})

    def start_right(u):
        for d in range(1, GROUP):
            r_copy(u, d).start()

    def c_copy(b):
        return pltpu.make_async_remote_copy(
            c_out.at[b], c_in.at[b], c_send.at[b], c_recv.at[b], device_id={"srf": other})

    def z_copy(b, d):
        to = lax.rem(team + d, teams)
        return pltpu.make_async_remote_copy(
            z_out.at[b, to], z_in.at[b, d], z_send.at[b, d], z_recv.at[b, d],
            device_id={"src": to * GROUP + place})

    def f_copy(b, d):
        to = partner(d)
        return pltpu.make_async_remote_copy(
            f_out.at[b, to], f_in.at[place, b], f_send.at[b, d], f_recv.at[b, d],
            device_id={"src": team * GROUP + to})

    def start_left(d, carry):
        l_copy(d).start()
        return carry

    lax.fori_loop(1, n, start_left, 0)

    fetches[4].wait()
    if row_count < ROW_TILE:
        lines[...] = jnp.zeros_like(lines)
    for side in range(2):
        for q in range(row_count):
            bands = spectrum(traces[q, side * half:(side + 1) * half]).astype(F32)
            for t in range(half // LANES):
                lines[side * (half // LANES) + t, pl.ds(q, values, stride=ROW_TILE), :] = (
                    bands[:, t * LANES:(t + 1) * LANES])
        for t in range(half // LANES):
            block = lines[side * (half // LANES) + t].astype(BF16)
            right[side, ..., t * LANES:(t + 1) * LANES] = block.reshape(
                GROUP, SLOTS, 2, ROW_TILE, LANES)
        for u in range(FIRST) if side == 0 else range(FIRST, EARLY):
            start_right(u)
        for b in range(SLOTS):
            r_in[side, b, :, place] = right[side, place, b]
    l_in[me] = left[me]

    def wait_left(d, carry):
        l_copy(d).wait_recv()
        return carry

    lax.fori_loop(1, n, wait_left, 0)
    for b in range(SLOTS):
        wide = l_in[:, b].astype(F32).reshape(n, 2, ROW_TILE // 2, rows)
        turned = jnp.concatenate([-wide[:, 1:2], wide[:, 0:1]], axis=1)
        l_turn[b] = turned.reshape(n * ROW_TILE, rows).astype(BF16)

    def multiply(u):
        side, b = units[u]
        for d in range(1, GROUP):
            r_copy(u, d).wait_recv()
        if EARLY <= u + AHEAD < len(units):
            start_right(u + AHEAD)
        straight = l_in[:, b].reshape(n * ROW_TILE, rows)
        real = r_in[side, b, 0].reshape(rows, half)
        imag = r_in[side, b, 1].reshape(rows, half)
        total = jnp.dot(straight, real, preferred_element_type=F32)
        part[b, side] = total + jnp.dot(l_turn[b], imag, preferred_element_type=F32)

        @pl.when(core != side)
        def _():
            c_out[b] = part[b, side].astype(BF16)
            c_copy(b).start()

    def add_cores(b):
        c_copy(b).wait_recv()
        total = part[b, core] + c_in[b].astype(F32)
        part[b, core] = total
        z_out[b] = total.astype(BF16).reshape(teams, rows, half)
        for d in range(1, teams):
            z_copy(b, d).start()

    def add_teams(b):
        total = part[b, core, pl.ds(pl.multiple_of(team * rows, rows), rows), :]
        for d in range(1, teams):
            z_copy(b, d).wait_recv()
            total += z_in[b, d].astype(F32)
        f_out[b] = total.astype(BF16).reshape(GROUP, ROW_TILE, half)
        for d in range(1, GROUP):
            f_copy(b, d).start()
        f_in[place, b] = f_out[b, place]

    for step in range(len(units) + GAP):
        if step < len(units):
            multiply(step)
        for lag, work in ((1, add_cores), (GAP, add_teams)):
            if 0 <= step - lag < len(units):
                side, b = units[step - lag]
                pl.when(core == side)(functools.partial(work, b))
    for b in range(SLOTS):
        for d in range(1, GROUP):
            f_copy(b, d).wait_recv()
    out[...] = f_in[...]

    def end_left(d, carry):
        l_copy(d).wait_send()
        return carry

    lax.fori_loop(1, n, end_left, 0)
    for b in range(SLOTS):
        c_copy(b).wait_send()
        for d in range(1, GROUP):
            r_copy(b, d).wait_send()
            r_copy(b + SLOTS, d).wait_send()
            f_copy(b, d).wait_send()
        for d in range(1, teams):
            z_copy(b, d).wait_send()


def band_of(n, left, right, surf_map, shot_map, table):
    teams = n // GROUP
    rows = GROUP * ROW_TILE
    receivers = right.shape[2]
    half = receivers // 2
    dma = pltpu.SemaphoreType.DMA
    vmem = pl.BlockSpec(memory_space=pltpu.VMEM)
    return pl.pallas_call(
        functools.partial(exchange, n),
        out_shape=jax.ShapeDtypeStruct((GROUP, SLOTS, ROW_TILE, half), BF16),
        in_specs=[pl.BlockSpec(memory_space=pltpu.HBM)] * 5,
        out_specs=vmem,
        scratch_shapes=[
            pltpu.VMEM(left.shape, BF16),
            pltpu.VMEM(right.shape[1:], BF16),
            pltpu.VMEM(surf_map.shape, jnp.int32),
            pltpu.VMEM(shot_map.shape, jnp.int32),
            pltpu.VMEM(table.shape, BF16),
            pltpu.VMEM((max(teams, receivers // LANES), 2 * BINS * ROW_TILE, LANES), F32),
            pltpu.VMEM((2, GROUP, SLOTS, 2, ROW_TILE, half), BF16),
            pltpu.VMEM((n, SLOTS, ROW_TILE, rows), BF16),
            pltpu.VMEM((2, SLOTS, 2, GROUP, ROW_TILE, half), BF16),
            pltpu.VMEM((n, SLOTS, ROW_TILE, rows), BF16),
            pltpu.VMEM((SLOTS, n * ROW_TILE, rows), BF16),
            pltpu.VMEM((SLOTS, 2, n * ROW_TILE, half), F32),
            pltpu.VMEM((SLOTS, n * ROW_TILE, half), BF16),
            pltpu.VMEM((SLOTS, n * ROW_TILE, half), BF16),
            pltpu.VMEM((SLOTS, teams, rows, half), BF16),
            pltpu.VMEM((SLOTS, teams, rows, half), BF16),
            pltpu.VMEM((SLOTS, GROUP, ROW_TILE, half), BF16),
            pltpu.VMEM((GROUP, SLOTS, ROW_TILE, half), BF16),
            dma((5,)),
            dma((2 * SLOTS, GROUP)), dma((2 * SLOTS, GROUP)),
            dma((n,)), dma((n,)),
            dma((SLOTS,)), dma((SLOTS,)),
            dma((SLOTS, teams)), dma((SLOTS, teams)),
            dma((SLOTS, GROUP)), dma((SLOTS, GROUP)),
        ],
        compiler_params=pltpu.CompilerParams(
            collective_id=0, has_side_effects=True, vmem_limit_bytes=48 * 2**20),
        cost_estimate=pl.CostEstimate(
            flops=2 * SLOTS * n * ROW_TILE * 2 * rows * receivers,
            bytes_accessed=2 * right.size * 2, transcendentals=0),
    )(left, right, surf_map, shot_map, table)


def local(n, left_traces, right_traces, surf_map, shot_map):
    sources, _, samples = left_traces.shape
    receivers = right_traces.shape[2]
    values = 2 * BINS
    forward, inverse = tables(samples)
    band = band_of(n, left_traces, right_traces, surf_map[None], shot_map[None], jnp.asarray(forward))
    band = band.reshape(values, sources, receivers // 2)
    result = [
        jnp.einsum("csr,ct->srt", band, inverse[part], preferred_element_type=F32)
        for part in (slice(None, values), slice(values, None))
    ]
    return (result[0] + result[1]).astype(BF16)


def solution(mesh):
    in_specs = (
        P(("grp", "src"), "srf", None),
        P("srf", "src", "grp", None),
        P(("grp", "srf")),
        P(("grp", "srf")),
    )
    out_specs = P(("grp", "src"), "srf", None)
    body = functools.partial(local, mesh.shape["src"])
    return jax.shard_map(body, mesh=mesh, in_specs=in_specs, out_specs=out_specs, check_vma=False)
```

```python
import functools
import math

import jax
import jax.numpy as jnp
import ml_dtypes
import numpy as np
from jax import lax
from jax.experimental import pallas as pl
from jax.experimental.pallas import tpu as pltpu
from jax.sharding import PartitionSpec as P

BINS = 40
GROUP = 8
SLOTS = BINS // GROUP
ROW_TILE = 16
LANES = 128
FIRST = 3
EARLY = 6
AHEAD = 4
GAP = 3
F32 = jnp.float32
BF16 = jnp.bfloat16


def split(table):
    high = table.astype(ml_dtypes.bfloat16)
    low = (table - high.astype(np.float64)).astype(ml_dtypes.bfloat16)
    return np.concatenate([high, low], axis=0)


def tables(samples):
    phase = np.arange(1, BINS + 1)[:, None] * np.arange(samples)[None, :] % samples
    angles = phase * (2.0 * math.pi / samples)
    forward = np.stack([np.cos(angles), -np.sin(angles)], axis=1).reshape(2 * BINS, samples)
    return split(forward), split(forward * (2.0 / samples))


NT = (((1,), (1,)), ((), ()))


def exchange(n, left_hbm, right_hbm, surf_hbm, shot_hbm, table_hbm, out, left_ref, traces, surf_ref,
             shot_ref, table_ref, lines, right, left,
             r_in, l_in, l_turn, part, c_in, z_out, z_in, f_out, f_in, fetch_sem,
             r_send, r_recv, l_send, l_recv, c_send, c_recv, z_send, z_recv, f_send, f_recv):
    teams = n // GROUP
    me = lax.axis_index("src")
    core = lax.axis_index("srf")
    other = 1 - core
    team = me // GROUP
    place = me % GROUP
    rows = GROUP * ROW_TILE
    half = part.shape[-1]
    values = 2 * BINS
    sources, half_size, _ = left_ref.shape
    row_count, receivers = right_hbm.shape[1:3]

    pairs = [(surf_hbm, surf_ref), (shot_hbm, shot_ref), (table_hbm, table_ref), (left_hbm, left_ref),
             (right_hbm.at[0], traces)]
    fetches = [pltpu.make_async_copy(a, b, fetch_sem.at[i]) for i, (a, b) in enumerate(pairs)]
    for fetch in fetches:
        fetch.start()

    barrier = pltpu.get_barrier_semaphore()

    def greet(d, carry):
        pl.semaphore_signal(barrier, inc=1, device_id={"src": lax.rem(me + d, n)})
        return carry

    lax.fori_loop(1, n, greet, 0)
    pl.semaphore_signal(barrier, inc=1, device_id={"srf": other})
    def spectrum(block):
        both = lax.dot_general(table_ref[...], block, NT, preferred_element_type=F32)
        return (both[:values] + both[values:]).astype(BF16)

    for fetch in fetches[:4]:
        fetch.wait()
    at = lax.broadcasted_iota(jnp.int32, (half_size, half_size), 0)
    surf_hot = (at == surf_ref[...]).astype(F32).astype(BF16)
    spot = lax.broadcasted_iota(jnp.int32, (teams * rows, half_size), 0)
    shot = shot_ref[...]
    shot_spot = shot // row_count * ROW_TILE + shot % row_count
    shot_hot = (spot == shot_spot).astype(F32).astype(BF16)
    move = lax.dot_general(surf_hot, shot_hot, NT, preferred_element_type=F32).astype(BF16)
    for s in range(sources):
        moved = jnp.dot(spectrum(left_ref[s]), move, preferred_element_type=F32)
        for t in range(teams):
            lines[t, pl.ds(s, values, stride=sources), :] = moved[:, t * rows:(t + 1) * rows]
    for t in range(teams):
        block = lines[t, :values * sources].astype(BF16)
        left[t * GROUP:(t + 1) * GROUP] = block.reshape(GROUP, SLOTS, ROW_TILE, rows)

    pl.semaphore_wait(barrier, n)

    def l_copy(d):
        to = lax.rem(me + d, n)
        return pltpu.make_async_remote_copy(
            left.at[to], l_in.at[me], l_send.at[d], l_recv.at[d], device_id={"src": to})

    units = [(part_index, b) for part_index in range(2) for b in range(SLOTS)]

    def partner(d):
        return sum((place // bit % 2 + d // bit % 2) % 2 * bit for bit in (1, 2, 4))

    def r_copy(u, d):
        to = partner(d)
        side, b = units[u]
        return pltpu.make_async_remote_copy(
            right.at[side, to, b], r_in.at[side, b, :, place], r_send.at[u, d], r_recv.at[u, d],
            device_id={"src": team * GROUP + to})

    def start_right(u):
        for d in range(1, GROUP):
            r_copy(u, d).start()

    def c_copy(b):
        return pltpu.make_async_remote_copy(
            part.at[b, other], c_in.at[b], c_send.at[b], c_recv.at[b], device_id={"srf": other})

    def z_copy(b, d):
        to = lax.rem(team + d, teams)
        return pltpu.make_async_remote_copy(
            z_out.at[b, to], z_in.at[b, d], z_send.at[b, d], z_recv.at[b, d],
            device_id={"src": to * GROUP + place})

    def f_copy(b, d):
        to = partner(d)
        return pltpu.make_async_remote_copy(
            f_out.at[b, to], f_in.at[place, b], f_send.at[b, d], f_recv.at[b, d],
            device_id={"src": team * GROUP + to})

    def start_left(d, carry):
        l_copy(d).start()
        return carry

    lax.fori_loop(1, n, start_left, 0)

    fetches[4].wait()
    if row_count < ROW_TILE:
        lines[...] = jnp.zeros_like(lines)
    for side in range(2):
        for q in range(row_count):
            bands = spectrum(traces[q, side * half:(side + 1) * half]).astype(F32)
            for t in range(half // LANES):
                lines[side * (half // LANES) + t, pl.ds(q, values, stride=ROW_TILE), :] = (
                    bands[:, t * LANES:(t + 1) * LANES])
        for t in range(half // LANES):
            block = lines[side * (half // LANES) + t].astype(BF16)
            right[side, ..., t * LANES:(t + 1) * LANES] = block.reshape(
                GROUP, SLOTS, 2, ROW_TILE, LANES)
        for u in range(FIRST) if side == 0 else range(FIRST, EARLY):
            start_right(u)
        for b in range(SLOTS):
            r_in[side, b, :, place] = right[side, place, b]
    l_in[me] = left[me]

    def wait_left(d, carry):
        l_copy(d).wait_recv()
        return carry

    lax.fori_loop(1, n, wait_left, 0)
    for b in range(SLOTS):
        wide = l_in[:, b].astype(F32).reshape(n, 2, ROW_TILE // 2, rows)
        turned = jnp.concatenate([-wide[:, 1:2], wide[:, 0:1]], axis=1)
        l_turn[b] = turned.reshape(n * ROW_TILE, rows).astype(BF16)

    def multiply(u):
        side, b = units[u]
        for d in range(1, GROUP):
            r_copy(u, d).wait_recv()
        if EARLY <= u + AHEAD < len(units):
            start_right(u + AHEAD)
        straight = l_in[:, b].reshape(n * ROW_TILE, rows)
        real = r_in[side, b, 0].reshape(rows, half)
        imag = r_in[side, b, 1].reshape(rows, half)
        total = jnp.dot(straight, real, preferred_element_type=F32)
        part[b, side] = total + jnp.dot(l_turn[b], imag, preferred_element_type=F32)

        @pl.when(core != side)
        def _():
            c_copy(b).start()

    def add_cores(b):
        c_copy(b).wait_recv()
        total = part[b, core] + c_in[b]
        part[b, core] = total
        z_out[b] = total.astype(BF16).reshape(teams, rows, half)
        for d in range(1, teams):
            z_copy(b, d).start()

    def add_teams(b):
        total = part[b, core, pl.ds(pl.multiple_of(team * rows, rows), rows), :]
        for d in range(1, teams):
            z_copy(b, d).wait_recv()
            total += z_in[b, d].astype(F32)
        f_out[b] = total.astype(BF16).reshape(GROUP, ROW_TILE, half)
        for d in range(1, GROUP):
            f_copy(b, d).start()
        f_in[place, b] = f_out[b, place]

    for step in range(len(units) + GAP):
        if step < len(units):
            multiply(step)
        for lag, work in ((1, add_cores), (GAP, add_teams)):
            if 0 <= step - lag < len(units):
                side, b = units[step - lag]
                pl.when(core == side)(functools.partial(work, b))
    for b in range(SLOTS):
        for d in range(1, GROUP):
            f_copy(b, d).wait_recv()
    out[...] = f_in[...]

    def end_left(d, carry):
        l_copy(d).wait_send()
        return carry

    lax.fori_loop(1, n, end_left, 0)
    for b in range(SLOTS):
        c_copy(b).wait_send()
        for d in range(1, GROUP):
            r_copy(b, d).wait_send()
            r_copy(b + SLOTS, d).wait_send()
            f_copy(b, d).wait_send()
        for d in range(1, teams):
            z_copy(b, d).wait_send()


def band_of(n, left, right, surf_map, shot_map, table):
    teams = n // GROUP
    rows = GROUP * ROW_TILE
    receivers = right.shape[2]
    half = receivers // 2
    dma = pltpu.SemaphoreType.DMA
    vmem = pl.BlockSpec(memory_space=pltpu.VMEM)
    return pl.pallas_call(
        functools.partial(exchange, n),
        out_shape=jax.ShapeDtypeStruct((GROUP, SLOTS, ROW_TILE, half), BF16),
        in_specs=[pl.BlockSpec(memory_space=pltpu.HBM)] * 5,
        out_specs=vmem,
        scratch_shapes=[
            pltpu.VMEM(left.shape, BF16),
            pltpu.VMEM(right.shape[1:], BF16),
            pltpu.VMEM(surf_map.shape, jnp.int32),
            pltpu.VMEM(shot_map.shape, jnp.int32),
            pltpu.VMEM(table.shape, BF16),
            pltpu.VMEM((max(teams, receivers // LANES), 2 * BINS * ROW_TILE, LANES), F32),
            pltpu.VMEM((2, GROUP, SLOTS, 2, ROW_TILE, half), BF16),
            pltpu.VMEM((n, SLOTS, ROW_TILE, rows), BF16),
            pltpu.VMEM((2, SLOTS, 2, GROUP, ROW_TILE, half), BF16),
            pltpu.VMEM((n, SLOTS, ROW_TILE, rows), BF16),
            pltpu.VMEM((SLOTS, n * ROW_TILE, rows), BF16),
            pltpu.VMEM((SLOTS, 2, n * ROW_TILE, half), F32),
            pltpu.VMEM((SLOTS, n * ROW_TILE, half), F32),
            pltpu.VMEM((SLOTS, teams, rows, half), BF16),
            pltpu.VMEM((SLOTS, teams, rows, half), BF16),
            pltpu.VMEM((SLOTS, GROUP, ROW_TILE, half), BF16),
            pltpu.VMEM((GROUP, SLOTS, ROW_TILE, half), BF16),
            dma((5,)),
            dma((2 * SLOTS, GROUP)), dma((2 * SLOTS, GROUP)),
            dma((n,)), dma((n,)),
            dma((SLOTS,)), dma((SLOTS,)),
            dma((SLOTS, teams)), dma((SLOTS, teams)),
            dma((SLOTS, GROUP)), dma((SLOTS, GROUP)),
        ],
        compiler_params=pltpu.CompilerParams(
            collective_id=0, has_side_effects=True, vmem_limit_bytes=48 * 2**20),
        cost_estimate=pl.CostEstimate(
            flops=2 * SLOTS * n * ROW_TILE * 2 * rows * receivers,
            bytes_accessed=2 * right.size * 2, transcendentals=0),
    )(left, right, surf_map, shot_map, table)


def local(n, left_traces, right_traces, surf_map, shot_map):
    sources, _, samples = left_traces.shape
    receivers = right_traces.shape[2]
    values = 2 * BINS
    forward, inverse = tables(samples)
    band = band_of(n, left_traces, right_traces, surf_map[None], shot_map[None], jnp.asarray(forward))
    band = band.reshape(values, sources, receivers // 2)
    result = [
        jnp.einsum("csr,ct->srt", band, inverse[part], preferred_element_type=F32)
        for part in (slice(None, values), slice(values, None))
    ]
    return (result[0] + result[1]).astype(BF16)


def solution(mesh):
    in_specs = (
        P(("grp", "src"), "srf", None),
        P("srf", "src", "grp", None),
        P(("grp", "srf")),
        P(("grp", "srf")),
    )
    out_specs = P(("grp", "src"), "srf", None)
    body = functools.partial(local, mesh.shape["src"])
    return jax.shard_map(body, mesh=mesh, in_specs=in_specs, out_specs=out_specs, check_vma=False)
```
